32 devices in a mesh: groups: 2 (over x), replica: 8 (over z, y), tensor: 2 (over core).
Axes of the slice: x: 2, y: 2, z: 4, core: 2. Of those that a mesh axis runs over, the one named last changes fastest.
Arguments:
- cache_keys: bfloat16 [192, 128, 2560], P(('groups', 'replica'), None, 'tensor'), parts along dimension 0, may hold values from -6 to 6
- cache_values: bfloat16 [192, 128, 2560], P(('groups', 'replica'), None, 'tensor'), parts along dimension 0, may hold values from -6 to 6
- lengths: int32 [192], P(('groups', 'replica')), parts along dimension 0, may hold values from 1 to 128, 6144 in all
- new_slot: int32 [192], P(('groups', 'replica')), parts along dimension 0, may hold values from 0 to 95, as said below
- query_raw: bfloat16 [192, 32, 2560], P(('groups', 'replica'), None, 'tensor'), parts along dimension 0, may hold values from -1000 to 1000
- block_keys_raw: bfloat16 [192, 32, 2560], P(('groups', 'replica'), None, 'tensor'), parts along dimension 0, may hold values from -1000 to 1000
- block_values: bfloat16 [192, 32, 2560], P(('groups', 'replica'), None, 'tensor'), parts along dimension 0, may hold values from -6 to 6
- query_gain: bfloat16 [2560], P('tensor'), may hold values from 0.5 to 1.5
- key_gain: bfloat16 [2560], P('tensor'), may hold values from 0.5 to 1.5
Outputs:
- attended: bfloat16 [192, 32, 2560], P(('groups', 'replica'), None, 'tensor'), parts along dimension 0
The draws below stay inside these ranges and needn't reach their ends.
There are 2 independent parts, one for each index of `groups`. The reference program is written for one: setup_inputs(seed, part) draws one part's arguments, and reference() takes and returns one part's arrays. A program takes and returns all parts, laid end to end along the dimension named above; an argument that names none is the same for every part. Nothing has to cross between parts.
Inputs may be any that keep to these rules, and one draw needn't show every extreme that they name: new_slot is a permutation; slot // 12 is a replica. Of one replica's streams at most 2 go to any one replica (its own included), and some pair of replicas reaches 2. Streams in the same slot position of different replicas go to different replicas.
All inputs are finite; a program needn't handle non-finite values. No bound on the sum of `lengths` on one device may be relied on, other than what follows from the above.
Results may differ from the reference program's by a relative error of at most 0.0083.
Values may be sent and summed in bfloat16 or wider, within the bound.
A program may use at most 128 MiB of HBM per device.

```python
import math
import jax
import jax.numpy as jnp
import numpy as np
from jax import lax

HEADS = 20
HEAD_DIM = 128
SLOTS = 12
CACHE = 128
BLOCK = 32
STREAMS = 96


def column_scales(key):
    full_width = HEADS * HEAD_DIM
    ramp = 1.0 + 2.0 * jnp.arange(full_width, dtype=jnp.float32) / (full_width - 1)
    return ramp * jnp.exp(2.3 * jax.random.uniform(jax.random.fold_in(key, 101), (full_width,)))


def rough_rows(key, row_count, top_scale):
    full_width = HEADS * HEAD_DIM
    shape = (STREAMS, row_count, full_width)
    normal_part = jax.random.normal(jax.random.fold_in(key, 1), shape)
    mixed = normal_part
    row_scale = jnp.exp(jnp.log(top_scale) * jax.random.uniform(jax.random.fold_in(key, 3), (STREAMS, row_count, 1)))
    return mixed * row_scale


def draw_new_slot(key, part):
    key = jax.random.fold_in(key, 3)
    replicas = STREAMS // SLOTS
    outer = jax.random.permutation(jax.random.fold_in(key, 1), replicas)
    inner = jax.random.permutation(jax.random.fold_in(key, 2), replicas)
    places = jax.vmap(lambda sub: jax.random.permutation(sub, SLOTS))(jax.random.split(jax.random.fold_in(key, 4), replicas))
    source = jnp.arange(replicas)[:, None]
    position = jnp.arange(SLOTS)[None, :]
    target = outer[(inner[source] + position) % replicas]
    local_place = places[target, position]
    return (target * SLOTS + local_place).reshape(-1).astype(jnp.int32)


def draw_query_raw(key, part):
    scales = column_scales(key)
    key = jax.random.fold_in(key, 5)
    rows = rough_rows(key, BLOCK, 10.0) * scales
    return jnp.clip(rows, -1000.0, 1000.0).astype(jnp.bfloat16)


def draw_block_keys_raw(key, part):
    scales = column_scales(key)
    key = jax.random.fold_in(key, 6)
    rows = rough_rows(key, BLOCK, 10.0) * scales
    return jnp.clip(rows, -1000.0, 1000.0).astype(jnp.bfloat16)


def block_scale(rng, shape, pieces, smallest, high):
    def one(dim, parts):
        draws = jax.random.uniform(jax.random.fold_in(jax.random.fold_in(rng, 6), dim), (parts,), jnp.float32, smallest / len(pieces), high / len(pieces))
        return jnp.repeat(jnp.exp(draws), shape[dim] // parts).reshape((-1,) + (1,) * (len(shape) - dim - 1))

    level = one(*pieces[0])
    for cut in pieces[1:]:
        level = level * one(*cut)
    return level


def split_up(count, total, bound, skew):
    portions = [(1 << 20) // math.isqrt(grade ** skew) + 1 for grade in range(2, count + 1)]
    surplus, holding = total - bound - (count - 1), [1] * (count - 1)
    while surplus > 0:
        free = [i for i in range(count - 1) if holding[i] < bound]
        whole, remaining = sum([portions[i] for i in free]), surplus
        for i in free:
            addition = min(bound - holding[i], max(1, remaining * portions[i] // whole), surplus)
            holding[i] = holding[i] + addition
            surplus = surplus - addition
    return np.array([bound] + holding)


def uneven_parts(rng, count, total, reach, lean):
    if count == 2:
        one = jax.random.randint(rng, (), max(1, total - reach), min(reach, total - 1) + 1)
        return jnp.stack([one, total - one])
    sizes = jnp.asarray(split_up(count, total, reach, lean), jnp.int32)
    pairs = (count - 1) // 2
    giver, sink = sizes[1:1 + 2 * pairs:2], sizes[2:2 + 2 * pairs:2]
    room = jnp.minimum(giver - 1, reach - sink)
    passed = jax.random.randint(jax.random.fold_in(rng, 1), (pairs,), 0, 1 << 20) % (room + 1)
    sizes = sizes.at[1:1 + 2 * pairs:2].set(giver - passed).at[2:2 + 2 * pairs:2].set(sink + passed)
    return sizes[jax.random.permutation(jax.random.fold_in(rng, 2), count)]


def noise(key, dims, spread, bound, pieces=(), kind=jnp.bfloat16):
    loudness = block_scale(key, dims, pieces, -0.22, 0.18) if pieces else 1.0
    array = jax.random.normal(key, dims, jnp.float32) * spread * loudness
    return jnp.minimum(jnp.maximum(array, -bound), bound).astype(kind)


def setup_inputs(seed: int = 0, part: int = 0) -> dict:
    streams_of = jax.random.split(jax.random.key(seed), 10)
    part_splits = jax.random.split(jax.random.fold_in(streams_of[9], part), 10)
    cache_keys = noise(part_splits[0], (STREAMS, CACHE, HEADS * HEAD_DIM), 1.0, 6.0, ((0, 8), (2, 2)))
    cache_values = noise(part_splits[1], (STREAMS, CACHE, HEADS * HEAD_DIM), 1.0, 6.0, ((0, 8), (2, 2)))
    lengths = uneven_parts(part_splits[2], STREAMS, STREAMS * CACHE // 2, CACHE, 2).astype(jnp.int32)
    new_slot = draw_new_slot(jax.random.fold_in(jax.random.fold_in(streams_of[9], part), 71), part)
    query_raw = draw_query_raw(jax.random.fold_in(jax.random.fold_in(streams_of[9], part), 71), part)
    block_keys_raw = draw_block_keys_raw(jax.random.fold_in(jax.random.fold_in(streams_of[9], part), 71), part)
    block_values = noise(part_splits[6], (STREAMS, BLOCK, HEADS * HEAD_DIM), 1.0, 6.0, ((0, 8), (2, 2)))
    query_gain = jnp.clip(1.0 + 0.1 * jax.random.normal(streams_of[7], (HEADS * HEAD_DIM,), jnp.float32), 0.5, 1.5).astype(jnp.bfloat16)
    key_gain = jnp.clip(1.0 + 0.1 * jax.random.normal(streams_of[8], (HEADS * HEAD_DIM,), jnp.float32), 0.5, 1.5).astype(jnp.bfloat16)
    return dict(cache_keys=cache_keys, cache_values=cache_values, lengths=lengths, new_slot=new_slot, query_raw=query_raw, block_keys_raw=block_keys_raw, block_values=block_values, query_gain=query_gain, key_gain=key_gain)


def normed_rows(raw, gain):
    values = raw.astype(jnp.float32)
    factor = lax.rsqrt(lax.optimization_barrier(jnp.mean(values * values, axis=-1, keepdims=True)) + 1e-06)
    return (values * factor * gain.astype(jnp.float32)).astype(jnp.bfloat16)

def reference(cache_keys, cache_values, lengths, new_slot, query_raw, block_keys_raw, block_values, query_gain, key_gain):
    full_width = HEADS * HEAD_DIM
    score_scale = HEAD_DIM ** (-0.5)
    query_normed = normed_rows(query_raw, query_gain)
    key_normed = normed_rows(block_keys_raw, key_gain)
    anchor = jnp.zeros((STREAMS,), jnp.int32).at[new_slot].set(jnp.arange(STREAMS, dtype=jnp.int32))

    def one_stream(slot_index):
        source = anchor[slot_index]
        query_heads = query_normed[slot_index].astype(jnp.float32).reshape(BLOCK, HEADS, HEAD_DIM)
        past_keys = cache_keys[source].astype(jnp.float32).reshape(CACHE, HEADS, HEAD_DIM)
        past_values = cache_values[source].astype(jnp.float32).reshape(CACHE, HEADS, HEAD_DIM)
        own_keys = key_normed[slot_index].astype(jnp.float32).reshape(BLOCK, HEADS, HEAD_DIM)
        own_values = block_values[slot_index].astype(jnp.float32).reshape(BLOCK, HEADS, HEAD_DIM)
        past_scores = jnp.einsum('qhd,khd->hqk', query_heads, past_keys) * score_scale
        valid = jnp.arange(CACHE, dtype=jnp.int32) < lengths[source]
        past_scores = jnp.where(valid[None, None, :], past_scores, -1e+30)
        own_scores = jnp.einsum('qhd,khd->hqk', query_heads, own_keys) * score_scale
        scores = jnp.concatenate([past_scores, own_scores], axis=-1)
        weights = jax.nn.softmax(scores, axis=-1).astype(jnp.bfloat16)
        all_values = jnp.concatenate([past_values, own_values], axis=0)
        result = jnp.einsum('hqk,khd->qhd', weights.astype(jnp.float32), all_values)
        return result.reshape(BLOCK, full_width).astype(jnp.bfloat16)
    return lax.map(one_stream, jnp.arange(STREAMS, dtype=jnp.int32))
```

```python
import jax
import jax.numpy as jnp
from jax import lax
from jax.sharding import PartitionSpec as P

HEAD_DIM = 128


def split_heads(source_rows):
    return source_rows.reshape(
        source_rows.shape[0], source_rows.shape[1], source_rows.shape[2] // HEAD_DIM, HEAD_DIM
    )


def pick_rows(selection, source_rows):
    flattened = source_rows.reshape(source_rows.shape[0], -1)
    picked = jnp.dot(selection, flattened, preferred_element_type=jnp.float32).astype(
        source_rows.dtype
    )
    return picked.reshape((selection.shape[0],) + source_rows.shape[1:])


def own_scores(queries, block_keys):
    return jnp.einsum(
        "sqhd,skhd->shqk",
        split_heads(queries),
        split_heads(block_keys),
        preferred_element_type=jnp.float32,
    ) * HEAD_DIM ** (-0.5)


def partial(scores, vals):
    row_max = jnp.max(scores, axis=-1, keepdims=True)
    weights = jnp.exp(scores - row_max)
    total = jnp.sum(weights, axis=-1, keepdims=True)
    result = jnp.einsum(
        "shqk,skhd->sqhd",
        (weights / total).astype(jnp.bfloat16),
        split_heads(vals),
        preferred_element_type=jnp.float32,
    )
    return result, (row_max + jnp.log(total))[..., 0]


def pick_exact(selection, rows):
    flattened = rows.reshape(rows.shape[0], -1)
    picked = jnp.dot(selection.astype(jnp.float32), flattened, precision=lax.Precision.HIGHEST)
    return picked.reshape((selection.shape[0],) + rows.shape[1:])


def local(
    cache_keys,
    cache_values,
    lengths,
    new_slot,
    query_raw,
    block_keys_raw,
    block_values,
    query_gain,
    key_gain,
):
    slot_count = cache_keys.shape[0]
    local_width = cache_keys.shape[2]
    full_width = local_width * lax.axis_size("tensor")
    peer_count = lax.axis_size("replica")
    own_index = lax.axis_index("replica")
    capacity = -(-slot_count // peer_count)
    query_float = query_raw.astype(jnp.float32)
    key_float = block_keys_raw.astype(jnp.float32)
    query_squares, key_squares = lax.psum(
        (jnp.sum(query_float * query_float, axis=-1), jnp.sum(key_float * key_float, axis=-1)),
        "tensor",
    )
    query_normed = (
        query_float
        * lax.rsqrt(query_squares / full_width + 1e-06)[..., None]
        * query_gain.astype(jnp.float32)
    ).astype(jnp.bfloat16)
    key_normed = (
        key_float
        * lax.rsqrt(key_squares / full_width + 1e-06)[..., None]
        * key_gain.astype(jnp.float32)
    ).astype(jnp.bfloat16)
    position = jnp.arange(slot_count, dtype=jnp.int32)
    bucket_ids = jnp.arange(peer_count * capacity, dtype=jnp.int32)
    dest_local = new_slot // slot_count
    earlier = (position[None, :] < position[:, None]) & (dest_local[None, :] == dest_local[:, None])
    rank_local = jnp.sum(earlier.astype(jnp.int32), axis=1)
    send_select = ((dest_local * capacity + rank_local)[None, :] == bucket_ids[:, None]).astype(
        jnp.bfloat16
    )
    all_slots = lax.all_gather(new_slot, "replica", axis=0, tiled=True)
    stream_total = all_slots.shape[0]
    dest_board = (all_slots // slot_count).reshape(peer_count, slot_count)
    matches = (dest_board[:, None, :] == dest_board[:, :, None]) & (
        position[None, None, :] < position[None, :, None]
    )
    rank_all = jnp.sum(matches.astype(jnp.int32), axis=2).reshape(stream_total)
    column = jnp.arange(stream_total, dtype=jnp.int32) // slot_count * capacity + rank_all
    arrive = (all_slots[None, :] == own_index * slot_count + position[:, None]).astype(jnp.float32)
    receive_select = jnp.dot(
        arrive,
        (column[:, None] == bucket_ids[None, :]).astype(jnp.float32),
        preferred_element_type=jnp.float32,
    ).astype(jnp.bfloat16)
    outgoing = pick_rows(receive_select.T, query_normed)
    arrived = lax.all_to_all(outgoing, "replica", split_axis=0, concat_axis=0, tiled=True)
    own_result, own_level = partial(own_scores(query_normed, key_normed), block_values)
    visitors = pick_rows(send_select.T, arrived)
    past_part = own_scores(visitors, cache_keys)
    valid = jnp.arange(cache_keys.shape[1], dtype=jnp.int32)[None, :] < lengths[:, None]
    past_part = jnp.where(valid[:, None, None, :], past_part, -1e30)
    past_result, past_level = partial(past_part, cache_values)
    past_result = past_result.astype(jnp.bfloat16).reshape(query_raw.shape)
    sent_result, sent_level = pick_rows(send_select, past_result), pick_exact(send_select, past_level)
    back_result, back_level = (
        lax.all_to_all(sent_result, "replica", split_axis=0, concat_axis=0, tiled=True),
        lax.all_to_all(sent_level, "replica", split_axis=0, concat_axis=0, tiled=True),
    )
    past_result = split_heads(pick_rows(receive_select, back_result)).astype(jnp.float32)
    past_level = pick_exact(receive_select, back_level)
    share = jax.nn.sigmoid(past_level - own_level).transpose(0, 2, 1)[..., None]
    result = own_result + share * (past_result - own_result)
    return result.reshape(query_raw.shape).astype(jnp.bfloat16)


def solution(mesh):
    in_specs = (
        P(("groups", "replica"), None, "tensor"),
        P(("groups", "replica"), None, "tensor"),
        P(("groups", "replica")),
        P(("groups", "replica")),
        P(("groups", "replica"), None, "tensor"),
        P(("groups", "replica"), None, "tensor"),
        P(("groups", "replica"), None, "tensor"),
        P("tensor"),
        P("tensor"),
    )
    out_specs = P(("groups", "replica"), None, "tensor")
    return jax.shard_map(local, mesh=mesh, in_specs=in_specs, out_specs=out_specs, check_vma=False)
```

```python
import functools

import jax
import jax.numpy as jnp
from jax import lax
from jax.experimental import pallas as pl
from jax.experimental.pallas import tpu as pltpu
from jax.sharding import PartitionSpec as P

HEAD_DIM = 128
PAIR = 2 * HEAD_DIM
LANES = 128
MESH = pl.DeviceIdType.MESH
F32 = jnp.float32
BF16 = jnp.bfloat16


def pair_attention(queries, keys, values, valid):
    rows = queries.shape[0]
    zeros = jnp.zeros((rows, HEAD_DIM), queries.dtype)
    diagonal = jnp.concatenate(
        [
            jnp.concatenate([queries[:, :HEAD_DIM], zeros], axis=1),
            jnp.concatenate([zeros, queries[:, HEAD_DIM:]], axis=1),
        ],
        axis=0,
    )
    scores = lax.dot_general(
        diagonal, keys, (((1,), (1,)), ((), ())), preferred_element_type=F32
    ) * HEAD_DIM ** (-0.5)
    if valid is not None:
        scores = jnp.where(valid, scores, -1e30)
    top = jnp.max(scores, axis=1, keepdims=True)
    weights = jnp.exp(scores - top)
    total = jnp.sum(weights, axis=1, keepdims=True)
    result = jnp.dot(weights.astype(BF16), values, preferred_element_type=F32)
    inverse = 1.0 / total
    first = result[:rows, :HEAD_DIM] * inverse[:rows]
    second = result[rows:, HEAD_DIM:] * inverse[rows:]
    level = top + jnp.log(total)
    return jnp.concatenate([first, second], axis=1), level[:rows], level[rows:]


def kernel(
    peers,
    capacity,
    full_width,
    row_ref,
    lengths_ref,
    query_hbm,
    key_hbm,
    value_hbm,
    cache_key_hbm,
    cache_value_hbm,
    query_gain_ref,
    key_gain_ref,
    out_ref,
    query,
    key,
    value,
    cache_key,
    cache_value,
    squares,
    squares_other,
    tables,
    picks_vmem,
    picks,
    query_out,
    query_in,
    result_out,
    result_in,
    own_result,
    own_level,
    load_sem,
    square_sem,
    table_send,
    table_recv,
    query_send,
    query_recv,
    result_send,
    result_recv,
):
    slots, block, width = query.shape
    pairs = width // PAIR
    me = lax.axis_index("replica")
    other = 1 - lax.axis_index("tensor")

    def peer(d):
        return lax.rem(me + d, peers)

    def order(k):
        half = (k + 1) // 2
        return jnp.where(lax.rem(k, 2) == 0, peers // 2 + half, peers // 2 - half)

    loads = [
        pltpu.make_async_copy(source, target, load_sem.at[n])
        for n, (source, target) in enumerate(
            (
                (query_hbm, query),
                (key_hbm, key),
                (value_hbm, value),
                (cache_key_hbm, cache_key),
                (cache_value_hbm, cache_value),
            )
        )
    ]
    for load in loads:
        load.start()

    barrier = pltpu.get_barrier_semaphore()
    pl.semaphore_signal(barrier, inc=1, device_id={"tensor": other}, device_id_type=MESH)

    def greet(d, carry):
        pl.semaphore_signal(barrier, inc=1, device_id={"replica": peer(d)}, device_id_type=MESH)
        return carry

    lax.fori_loop(1, peers, greet, 0)
    tables[0] = row_ref[...]
    pl.semaphore_wait(barrier, peers)

    def table_copy(d):
        return pltpu.make_async_remote_copy(
            src_ref=row_ref,
            dst_ref=tables.at[d],
            send_sem=table_send.at[d],
            recv_sem=table_recv.at[d],
            device_id={"replica": peer(d)},
            device_id_type=MESH,
        )

    lax.fori_loop(1, peers, lambda d, carry: (table_copy(d).start(), carry)[1], 0)

    lane = lax.broadcasted_iota(jnp.int32, (block, LANES), 1)
    sums = jnp.zeros((block, LANES), F32)
    for ref, load, offset in ((query, loads[0], 0), (key, loads[1], LANES // 2)):
        load.wait()
        for i in range(slots):
            rows = ref[i].astype(F32)
            total = jnp.sum(rows * rows, axis=1, keepdims=True)
            sums = jnp.where(lane == offset + i, total, sums)
    squares[...] = sums
    exchange = pltpu.make_async_remote_copy(
        src_ref=squares,
        dst_ref=squares_other,
        send_sem=square_sem.at[0],
        recv_sem=square_sem.at[1],
        device_id={"tensor": other},
        device_id_type=MESH,
    )
    exchange.start()

    lax.fori_loop(1, peers, lambda d, carry: (table_copy(d).wait_recv(), carry)[1], 0)
    board = tables[:, 0, :]
    shape = board.shape
    column = lax.broadcasted_iota(jnp.int32, shape, 1)
    sender = lax.broadcasted_iota(jnp.int32, shape, 0)
    mirrored = jnp.where(sender == 0, 0, peers - sender)
    own_row = jnp.broadcast_to(tables[0][0:1], shape)
    back_base = lax.rem(me - sender + peers, peers) * slots
    chosen = jnp.zeros(shape, jnp.int32)
    places = jnp.zeros(shape, jnp.int32)
    mine = (board >= me * slots) & (board < me * slots + slots)
    theirs = (own_row >= back_base) & (own_row < back_base + slots)
    for r in range(capacity):
        first = jnp.min(jnp.where(mine, column, LANES), axis=1, keepdims=True)
        now = mine & (column == first)
        local = jnp.max(jnp.where(now, board - me * slots, 0), axis=1, keepdims=True)
        chosen = jnp.where(column == r, local, chosen)
        places = jnp.where(now, mirrored * capacity + r, places)
        mine = mine & (column != first)
        first = jnp.min(jnp.where(theirs, column, LANES), axis=1, keepdims=True)
        chosen = jnp.where(column == capacity + r, jnp.where(first == LANES, 0, first), chosen)
        theirs = theirs & (column != first)
    for i in range(slots):
        matching = jnp.where(board == me * slots + i, places, 0)
        place = jnp.max(jnp.max(matching, axis=1, keepdims=True), axis=0, keepdims=True)
        chosen = jnp.where(column == 2 * capacity + i, place, chosen)
    picks_vmem[...] = chosen
    to_scalars = pltpu.make_async_copy(picks_vmem, picks, load_sem.at[5])
    to_scalars.start()

    exchange.wait()
    factors = lax.rsqrt((squares[...] + squares_other[...]) / full_width + 1e-06)
    for i in range(slots):
        query[i] = (
            query[i].astype(F32) * factors[:, i : i + 1] * query_gain_ref[...].astype(F32)
        ).astype(BF16)
    to_scalars.wait()

    def query_copy(d):
        return pltpu.make_async_remote_copy(
            src_ref=query_out.at[d],
            dst_ref=query_in.at[d],
            send_sem=query_send.at[d],
            recv_sem=query_recv.at[d],
            device_id={"replica": peer(d)},
            device_id_type=MESH,
        )

    def result_copy(d):
        return pltpu.make_async_remote_copy(
            src_ref=result_out.at[d],
            dst_ref=result_in.at[d],
            send_sem=result_send.at[d],
            recv_sem=result_recv.at[d],
            device_id={"replica": lax.rem(me - d + peers, peers)},
            device_id_type=MESH,
        )

    def send_queries(k, carry):
        d = order(k)
        for r in range(capacity):
            query_out[d, r] = query[picks[peers - d, r]]
        query_copy(d).start()
        return carry

    lax.fori_loop(0, peers - 1, send_queries, 0)

    cached = cache_key.shape[1]
    position = lax.broadcasted_iota(jnp.int32, (2 * block, cached), 1)

    def visit(d, r, fetch, target):
        g = picks[d, capacity + r]
        valid = position < lengths_ref[g]
        levels = jnp.zeros((block, LANES), F32)
        for c in range(pairs):
            part = slice(c * PAIR, (c + 1) * PAIR)
            result, even, odd = pair_attention(
                fetch(part), cache_key[g, :, part], cache_value[g, :, part], valid
            )
            target[d, r, :, part] = result.astype(BF16)
            levels = jnp.where(lane % 32 == 2 * c, even, levels)
            levels = jnp.where(lane % 32 == 2 * c + 1, odd, levels)
        high = levels.astype(BF16).astype(F32)
        middle = (levels - high).astype(BF16).astype(F32)
        low = levels - high - middle
        pieces = jnp.where(lane < 32, high, jnp.where(lane < 64, middle, low))
        target[d, r, :, width:] = pieces.astype(BF16)

    def own_block(i, carry):
        levels = jnp.zeros((block, LANES), F32)
        for c in range(pairs):
            part = slice(c * PAIR, (c + 1) * PAIR)
            result, even, odd = pair_attention(
                query[i, :, part], key[i, :, part], value[i, :, part], None
            )
            own_result[i, :, part] = result
            levels = jnp.where(lane == 2 * c, even, levels)
            levels = jnp.where(lane == 2 * c + 1, odd, levels)
        own_level[i] = levels
        return carry

    for i in range(slots):
        at = LANES // 2 + i
        key[i] = (
            key[i].astype(F32) * factors[:, at : at + 1] * key_gain_ref[...].astype(F32)
        ).astype(BF16)
    for load in loads[2:]:
        load.wait()
    for r in range(capacity):
        i = picks[0, r]
        visit(0, r, lambda part: query[i, :, part], result_in)
    lax.fori_loop(0, slots, own_block, 0)

    def serve(k, carry):
        d = order(k)
        query_copy(d).wait_recv()
        for r in range(capacity):
            visit(d, r, lambda part: query_in[d, r, :, part], result_out)
        result_copy(d).start()
        return carry

    lax.fori_loop(0, peers - 1, serve, 0)
    lax.fori_loop(1, peers, lambda d, carry: (result_copy(d).wait_recv(), carry)[1], 0)

    def combine(i, carry):
        at = picks[0, 2 * capacity + i]
        from_peer, r = at // capacity, lax.rem(at, capacity)
        pieces = result_in[from_peer, r, :, width:].astype(F32)
        level = pieces + pltpu.roll(pieces, LANES - 32, 1) + pltpu.roll(pieces, LANES - 64, 1)
        share = 1.0 / (1.0 + jnp.exp(own_level[i] - level))
        for h in range(width // HEAD_DIM):
            part = slice(h * HEAD_DIM, (h + 1) * HEAD_DIM)
            own = own_result[i, :, part]
            past = result_in[from_peer, r, :, part].astype(F32)
            out_ref[i, :, part] = (own + share[:, h : h + 1] * (past - own)).astype(BF16)
        return carry

    lax.fori_loop(0, slots, combine, 0)

    def finish_sends(d, carry):
        table_copy(d).wait_send()
        query_copy(d).wait_send()
        result_copy(d).wait_send()
        return carry

    lax.fori_loop(1, peers, finish_sends, 0)


def local(
    cache_keys,
    cache_values,
    lengths,
    new_slot,
    query_raw,
    block_keys_raw,
    block_values,
    query_gain,
    key_gain,
):
    slots, block, width = query_raw.shape
    cached = cache_keys.shape[1]
    peers = lax.axis_size("replica")
    capacity = -(-slots // peers)
    full_width = width * lax.axis_size("tensor")
    row = jnp.broadcast_to(
        jnp.pad(new_slot, (0, LANES - slots), constant_values=-1)[None], (8, LANES)
    )
    vmem = pl.BlockSpec(memory_space=pltpu.VMEM)
    smem = pl.BlockSpec(memory_space=pltpu.SMEM)
    hbm = pl.BlockSpec(memory_space=pl.ANY)
    message = (peers, capacity, block, width)
    answer = (peers, capacity, block, width + LANES)
    dma = pltpu.SemaphoreType.DMA
    return pl.pallas_call(
        functools.partial(kernel, peers, capacity, full_width),
        out_shape=jax.ShapeDtypeStruct(query_raw.shape, BF16),
        in_specs=[vmem, smem, hbm, hbm, hbm, hbm, hbm, vmem, vmem],
        out_specs=vmem,
        scratch_shapes=[
            pltpu.VMEM(query_raw.shape, BF16),
            pltpu.VMEM(query_raw.shape, BF16),
            pltpu.VMEM(query_raw.shape, BF16),
            pltpu.VMEM(cache_keys.shape, BF16),
            pltpu.VMEM(cache_keys.shape, BF16),
            pltpu.VMEM((block, LANES), F32),
            pltpu.VMEM((block, LANES), F32),
            pltpu.VMEM((peers, 8, LANES), jnp.int32),
            pltpu.VMEM((peers, LANES), jnp.int32),
            pltpu.SMEM((peers, LANES), jnp.int32),
            pltpu.VMEM(message, BF16),
            pltpu.VMEM(message, BF16),
            pltpu.VMEM(answer, BF16),
            pltpu.VMEM(answer, BF16),
            pltpu.VMEM(query_raw.shape, F32),
            pltpu.VMEM((slots, block, LANES), F32),
            dma((6,)),
            dma((2,)),
            dma((peers,)),
            dma((peers,)),
            dma((peers,)),
            dma((peers,)),
            dma((peers,)),
            dma((peers,)),
        ],
        compiler_params=pltpu.CompilerParams(
            collective_id=0, has_side_effects=True, vmem_limit_bytes=48 * 1024 * 1024
        ),
        cost_estimate=pl.CostEstimate(
            flops=4 * slots * block * (cached + block) * width,
            bytes_accessed=4 * cache_keys.size + 8 * query_raw.size,
            transcendentals=slots * block * (cached + block) * width // HEAD_DIM,
        ),
    )(
        row,
        lengths,
        query_raw,
        block_keys_raw,
        block_values,
        cache_keys,
        cache_values,
        query_gain[None],
        key_gain[None],
    )


def solution(mesh):
    in_specs = (
        P(("groups", "replica"), None, "tensor"),
        P(("groups", "replica"), None, "tensor"),
        P(("groups", "replica")),
        P(("groups", "replica")),
        P(("groups", "replica"), None, "tensor"),
        P(("groups", "replica"), None, "tensor"),
        P(("groups", "replica"), None, "tensor"),
        P("tensor"),
        P("tensor"),
    )
    out_specs = P(("groups", "replica"), None, "tensor")
    return jax.shard_map(local, mesh=mesh, in_specs=in_specs, out_specs=out_specs, check_vma=False)
```

```python
import functools

import jax
import jax.numpy as jnp
from jax import lax
from jax.experimental import pallas as pl
from jax.experimental.pallas import tpu as pltpu
from jax.sharding import PartitionSpec as P

HEAD_DIM = 128
PAIR = 2 * HEAD_DIM
LANES = 128
MESH = pl.DeviceIdType.MESH
F32 = jnp.float32
BF16 = jnp.bfloat16


def pair_attention(queries, keys, values, valid):
    rows = queries.shape[0]
    zeros = jnp.zeros((rows, HEAD_DIM), queries.dtype)
    diagonal = jnp.concatenate(
        [
            jnp.concatenate([queries[:, :HEAD_DIM], zeros], axis=1),
            jnp.concatenate([zeros, queries[:, HEAD_DIM:]], axis=1),
        ],
        axis=0,
    )
    scores = lax.dot_general(
        diagonal, keys, (((1,), (1,)), ((), ())), preferred_element_type=F32
    ) * HEAD_DIM ** (-0.5)
    if valid is not None:
        scores = jnp.where(valid, scores, -1e30)
    top = jnp.max(scores, axis=1, keepdims=True)
    weights = jnp.exp(scores - top)
    total = jnp.sum(weights, axis=1, keepdims=True)
    result = jnp.dot(weights.astype(BF16), values, preferred_element_type=F32)
    inverse = 1.0 / total
    first = result[:rows, :HEAD_DIM] * inverse[:rows]
    second = result[rows:, HEAD_DIM:] * inverse[rows:]
    level = top + jnp.log(total)
    return jnp.concatenate([first, second], axis=1), level[:rows], level[rows:]


def kernel(
    peers,
    capacity,
    full_width,
    new_slot_ref,
    lengths_ref,
    query_hbm,
    key_hbm,
    value_hbm,
    cache_key_hbm,
    cache_value_hbm,
    query_gain_ref,
    key_gain_ref,
    out_ref,
    query,
    key,
    value,
    cache_key,
    cache_value,
    squares,
    squares_other,
    row,
    tables,
    sender_vmem,
    sender_picks,
    picks_vmem,
    picks,
    query_out,
    query_in,
    result_out,
    result_in,
    level_out,
    level_in,
    own_result,
    own_level,
    load_sem,
    square_sem,
    table_send,
    table_recv,
    query_send,
    query_recv,
    result_send,
    result_recv,
    level_send,
    level_recv,
):
    slots, block, width = query.shape
    pairs = width // PAIR
    me = lax.axis_index("replica")
    other = 1 - lax.axis_index("tensor")

    def peer(d):
        return lax.rem(me + d, peers)

    def order(k):
        half = (k + 1) // 2
        return jnp.where(lax.rem(k, 2) == 0, peers // 2 + half, peers // 2 - half)

    loads = [
        pltpu.make_async_copy(source, target, load_sem.at[n])
        for n, (source, target) in enumerate(
            (
                (query_hbm, query),
                (key_hbm, key),
                (value_hbm, value),
                (cache_key_hbm, cache_key),
                (cache_value_hbm, cache_value),
            )
        )
    ]
    loads[0].start()

    barrier = pltpu.get_barrier_semaphore()
    pl.semaphore_signal(barrier, inc=1, device_id={"tensor": other}, device_id_type=MESH)

    def greet(d, carry):
        pl.semaphore_signal(barrier, inc=1, device_id={"replica": peer(d)}, device_id_type=MESH)
        return carry

    lax.fori_loop(1, peers, greet, 0)
    tile_lane = lax.broadcasted_iota(jnp.int32, row.shape, 1)
    own_slots = jnp.full(row.shape, -1, jnp.int32)
    for j in range(slots):
        own_slots = jnp.where(tile_lane == j, new_slot_ref[j], own_slots)
    row[...] = own_slots
    tables[0] = own_slots
    pl.semaphore_wait(barrier, peers)

    def table_copy(d):
        return pltpu.make_async_remote_copy(
            src_ref=row,
            dst_ref=tables.at[d],
            send_sem=table_send.at[d],
            recv_sem=table_recv.at[d],
            device_id={"replica": peer(d)},
            device_id_type=MESH,
        )

    lax.fori_loop(1, peers, lambda d, carry: (table_copy(d).start(), carry)[1], 0)

    lane = lax.broadcasted_iota(jnp.int32, (block, LANES), 1)

    def sums_of(ref):
        sums = jnp.zeros((block, LANES), F32)
        for i in range(slots):
            rows = ref[i].astype(F32)
            sums = jnp.where(lane == i, jnp.sum(rows * rows, axis=1, keepdims=True), sums)
        return sums

    def exchange(n):
        return pltpu.make_async_remote_copy(
            src_ref=squares.at[n],
            dst_ref=squares_other.at[n],
            send_sem=square_sem.at[n, 0],
            recv_sem=square_sem.at[n, 1],
            device_id={"tensor": other},
            device_id_type=MESH,
        )

    def normalise(n, ref, gain_ref):
        exchange(n).wait()
        factors = lax.rsqrt((squares[n] + squares_other[n]) / full_width + 1e-06)
        gain = gain_ref[...].astype(F32).reshape(1, width)
        for i in range(slots):
            ref[i] = (ref[i].astype(F32) * factors[:, i : i + 1] * gain).astype(BF16)

    loads[0].wait()
    for load in loads[1:]:
        load.start()
    squares[0] = sums_of(query)
    exchange(0).start()

    lax.fori_loop(1, peers, lambda d, carry: (table_copy(d).wait_recv(), carry)[1], 0)
    board = tables[:, 0, :]
    shape = board.shape
    column = lax.broadcasted_iota(jnp.int32, shape, 1)
    sender = lax.broadcasted_iota(jnp.int32, shape, 0)
    mirrored = jnp.where(sender == 0, 0, peers - sender)
    mine = (board >= me * slots) & (board < me * slots + slots)
    chosen = jnp.zeros(shape, jnp.int32)
    places = jnp.zeros(shape, jnp.int32)
    for r in range(capacity):
        first = jnp.min(jnp.where(mine, column, LANES), axis=1, keepdims=True)
        now = mine & (column == first)
        local = jnp.max(jnp.where(now, board - me * slots, 0), axis=1, keepdims=True)
        chosen = jnp.where(column == r, local, chosen)
        places = jnp.where(now, mirrored * capacity + r, places)
        mine = mine & (column != first)
    sender_vmem[...] = chosen
    sender_scalars = pltpu.make_async_copy(sender_vmem, sender_picks, load_sem.at[5])
    sender_scalars.start()
    normalise(0, query, query_gain_ref)
    sender_scalars.wait()

    def query_copy(d):
        return pltpu.make_async_remote_copy(
            src_ref=query_out.at[d],
            dst_ref=query_in.at[d],
            send_sem=query_send.at[d],
            recv_sem=query_recv.at[d],
            device_id={"replica": peer(d)},
            device_id_type=MESH,
        )

    def result_copy(d):
        return pltpu.make_async_remote_copy(
            src_ref=result_out.at[d],
            dst_ref=result_in.at[d],
            send_sem=result_send.at[d],
            recv_sem=result_recv.at[d],
            device_id={"replica": lax.rem(me - d + peers, peers)},
            device_id_type=MESH,
        )

    def level_copy(d):
        return pltpu.make_async_remote_copy(
            src_ref=level_out.at[d],
            dst_ref=level_in.at[d],
            send_sem=level_send.at[d],
            recv_sem=level_recv.at[d],
            device_id={"replica": lax.rem(me - d + peers, peers)},
            device_id_type=MESH,
        )

    def send_queries(k, carry):
        d = order(k)
        for r in range(capacity):
            query_out[d, r] = query[sender_picks[peers - d, r]]
        query_copy(d).start()
        return carry

    lax.fori_loop(0, peers - 1, send_queries, 0)

    own_row = jnp.broadcast_to(tables[0][0:1], shape)
    back_base = lax.rem(me - sender + peers, peers) * slots
    theirs = (own_row >= back_base) & (own_row < back_base + slots)
    chosen = jnp.zeros(shape, jnp.int32)
    for r in range(capacity):
        first = jnp.min(jnp.where(theirs, column, LANES), axis=1, keepdims=True)
        chosen = jnp.where(column == r, jnp.where(first == LANES, 0, first), chosen)
        theirs = theirs & (column != first)
    for i in range(slots):
        matching = jnp.where(board == me * slots + i, places, 0)
        place = jnp.max(jnp.max(matching, axis=1, keepdims=True), axis=0, keepdims=True)
        chosen = jnp.where(column == capacity + i, place, chosen)
    picks_vmem[...] = chosen
    scalars = pltpu.make_async_copy(picks_vmem, picks, load_sem.at[6])
    scalars.start()
    loads[1].wait()
    squares[1] = sums_of(key)
    exchange(1).start()
    normalise(1, key, key_gain_ref)
    scalars.wait()
    for load in loads[2:]:
        load.wait()

    cached = cache_key.shape[1]
    position = lax.broadcasted_iota(jnp.int32, (2 * block, cached), 1)
    quarter = block // 4

    def visit(d, fetch, target, target_level):
        levels = jnp.zeros((block, LANES), F32)
        for r in range(capacity):
            g = picks[d, r]
            valid = position < lengths_ref[g]
            for c in range(pairs):
                part = slice(c * PAIR, (c + 1) * PAIR)
                result, even, odd = pair_attention(
                    fetch(r, part), cache_key[g, :, part], cache_value[g, :, part], valid
                )
                target[d, r, :, part] = result.astype(BF16)
                levels = jnp.where(lane == 16 * r + 2 * c, even, levels)
                levels = jnp.where(lane == 16 * r + 2 * c + 1, odd, levels)
        folded = levels[:quarter]
        for j in range(1, 4):
            folded = folded + pltpu.roll(levels[j * quarter : (j + 1) * quarter], 32 * j, 1)
        target_level[d] = folded

    def own_block(i, carry):
        levels = jnp.zeros((block, LANES), F32)
        for c in range(pairs):
            part = slice(c * PAIR, (c + 1) * PAIR)
            result, even, odd = pair_attention(
                query[i, :, part], key[i, :, part], value[i, :, part], None
            )
            own_result[i, :, part] = result
            levels = jnp.where(lane % 16 == 2 * c, even, levels)
            levels = jnp.where(lane % 16 == 2 * c + 1, odd, levels)
        own_level[i] = levels
        return carry

    def combine(d):
        folded = level_in[d]
        levels = jnp.concatenate(
            [folded] + [pltpu.roll(folded, LANES - 32 * j, 1) for j in range(1, 4)], axis=0
        )
        for r in range(capacity):
            i = sender_picks[lax.rem(peers - d, peers), r]
            share = 1.0 / (1.0 + jnp.exp(own_level[i] - levels))
            for h in range(width // HEAD_DIM):
                part = slice(h * HEAD_DIM, (h + 1) * HEAD_DIM)
                own = own_result[i, :, part]
                past = result_in[d, r, :, part].astype(F32)
                at = 16 * r + h
                mixed = own + share[:, at : at + 1] * (past - own)
                result_in[d, r, :, part] = mixed.astype(BF16)

    visit(0, lambda r, part: query[sender_picks[0, r], :, part], result_in, level_in)
    lax.fori_loop(0, slots, own_block, 0)

    def serve(k, carry):
        d = order(k)
        query_copy(d).wait_recv()
        visit(d, lambda r, part: query_in[d, r, :, part], result_out, level_out)
        level_copy(d).start()
        result_copy(d).start()
        return carry

    lax.fori_loop(0, peers - 1, serve, 0)
    combine(0)

    def collect(k, carry):
        d = order(k)
        level_copy(d).wait_recv()
        result_copy(d).wait_recv()
        combine(d)
        return carry

    lax.fori_loop(0, peers - 1, collect, 0)

    for i in range(slots):
        at = picks[0, capacity + i]
        out_ref[i] = result_in[at // capacity, lax.rem(at, capacity)]

    def finish_sends(d, carry):
        table_copy(d).wait_send()
        query_copy(d).wait_send()
        level_copy(d).wait_send()
        result_copy(d).wait_send()
        return carry

    lax.fori_loop(1, peers, finish_sends, 0)


def local(
    cache_keys,
    cache_values,
    lengths,
    new_slot,
    query_raw,
    block_keys_raw,
    block_values,
    query_gain,
    key_gain,
):
    slots, block, width = query_raw.shape
    cached = cache_keys.shape[1]
    peers = lax.axis_size("replica")
    capacity = -(-slots // peers)
    full_width = width * lax.axis_size("tensor")
    vmem = pl.BlockSpec(memory_space=pltpu.VMEM)
    smem = pl.BlockSpec(memory_space=pltpu.SMEM)
    hbm = pl.BlockSpec(memory_space=pl.ANY)
    message = (peers, capacity, block, width)
    level = (peers, block // 4, LANES)
    dma = pltpu.SemaphoreType.DMA
    return pl.pallas_call(
        functools.partial(kernel, peers, capacity, full_width),
        out_shape=jax.ShapeDtypeStruct(query_raw.shape, BF16),
        in_specs=[smem, smem, hbm, hbm, hbm, hbm, hbm, vmem, vmem],
        out_specs=vmem,
        scratch_shapes=[
            pltpu.VMEM(query_raw.shape, BF16),
            pltpu.VMEM(query_raw.shape, BF16),
            pltpu.VMEM(query_raw.shape, BF16),
            pltpu.VMEM(cache_keys.shape, BF16),
            pltpu.VMEM(cache_keys.shape, BF16),
            pltpu.VMEM((2, block, LANES), F32),
            pltpu.VMEM((2, block, LANES), F32),
            pltpu.VMEM((8, LANES), jnp.int32),
            pltpu.VMEM((peers, 8, LANES), jnp.int32),
            pltpu.VMEM((peers, LANES), jnp.int32),
            pltpu.SMEM((peers, LANES), jnp.int32),
            pltpu.VMEM((peers, LANES), jnp.int32),
            pltpu.SMEM((peers, LANES), jnp.int32),
            pltpu.VMEM(message, BF16),
            pltpu.VMEM(message, BF16),
            pltpu.VMEM(message, BF16),
            pltpu.VMEM(message, BF16),
            pltpu.VMEM(level, F32),
            pltpu.VMEM(level, F32),
            pltpu.VMEM(query_raw.shape, F32),
            pltpu.VMEM((slots, block, LANES), F32),
            dma((7,)),
            dma((2, 2)),
            dma((peers,)),
            dma((peers,)),
            dma((peers,)),
            dma((peers,)),
            dma((peers,)),
            dma((peers,)),
            dma((peers,)),
            dma((peers,)),
        ],
        compiler_params=pltpu.CompilerParams(
            collective_id=0, has_side_effects=True, vmem_limit_bytes=60 * 1024 * 1024
        ),
        cost_estimate=pl.CostEstimate(
            flops=4 * slots * block * (cached + block) * width,
            bytes_accessed=4 * cache_keys.size + 8 * query_raw.size,
            transcendentals=slots * block * (cached + block) * width // HEAD_DIM,
        ),
    )(
        new_slot,
        lengths,
        query_raw,
        block_keys_raw,
        block_values,
        cache_keys,
        cache_values,
        query_gain,
        key_gain,
    )


def solution(mesh):
    in_specs = (
        P(("groups", "replica"), None, "tensor"),
        P(("groups", "replica"), None, "tensor"),
        P(("groups", "replica")),
        P(("groups", "replica")),
        P(("groups", "replica"), None, "tensor"),
        P(("groups", "replica"), None, "tensor"),
        P(("groups", "replica"), None, "tensor"),
        P("tensor"),
        P("tensor"),
    )
    out_specs = P(("groups", "replica"), None, "tensor")
    return jax.shard_map(local, mesh=mesh, in_specs=in_specs, out_specs=out_specs, check_vma=False)
```

```python
import functools

import jax
import jax.numpy as jnp
from jax import lax
from jax.experimental import pallas as pl
from jax.experimental.pallas import tpu as pltpu
from jax.sharding import PartitionSpec as P

HEAD_DIM = 128
PAIR = 2 * HEAD_DIM
LANES = 128
MESH = pl.DeviceIdType.MESH
F32 = jnp.float32
BF16 = jnp.bfloat16


def pair_attention(queries, keys, values, valid):
    rows = queries.shape[0]
    zeros = jnp.zeros((rows, HEAD_DIM), queries.dtype)
    diagonal = jnp.concatenate(
        [
            jnp.concatenate([queries[:, :HEAD_DIM], zeros], axis=1),
            jnp.concatenate([zeros, queries[:, HEAD_DIM:]], axis=1),
        ],
        axis=0,
    )
    scores = lax.dot_general(
        diagonal, keys, (((1,), (1,)), ((), ())), preferred_element_type=F32
    ) * HEAD_DIM ** (-0.5)
    if valid is not None:
        scores = jnp.where(valid, scores, -1e30)
    top = jnp.max(scores, axis=1, keepdims=True)
    weights = jnp.exp(scores - top)
    total = jnp.sum(weights, axis=1, keepdims=True)
    result = jnp.dot(weights.astype(BF16), values, preferred_element_type=F32)
    inverse = 1.0 / total
    first = result[:rows, :HEAD_DIM] * inverse[:rows]
    second = result[rows:, HEAD_DIM:] * inverse[rows:]
    level = top + jnp.log(total)
    return jnp.concatenate([first, second], axis=1), level[:rows], level[rows:]


def kernel(
    peers,
    capacity,
    full_width,
    new_slot_ref,
    lengths_ref,
    query_hbm,
    key_hbm,
    value_hbm,
    cache_key_hbm,
    cache_value_hbm,
    query_gain_ref,
    key_gain_ref,
    out_ref,
    query,
    key,
    value,
    cache_key,
    cache_value,
    squares,
    squares_other,
    row,
    tables,
    sender_vmem,
    sender_picks,
    picks_vmem,
    picks,
    query_out,
    query_in,
    result_out,
    result_in,
    level_out,
    level_in,
    own_result,
    own_level,
    load_sem,
    square_sem,
    table_send,
    table_recv,
    query_send,
    query_recv,
    result_send,
    result_recv,
    level_send,
    level_recv,
):
    slots, block, width = query.shape
    pairs = width // PAIR
    me = lax.axis_index("replica")
    other = 1 - lax.axis_index("tensor")

    def peer(d):
        partner, bit = 0, 1
        while bit < peers:
            partner = partner + lax.rem(me // bit + d // bit, 2) * bit
            bit *= 2
        return partner

    half, quarter = peers // 2, peers // 4

    loads = [
        pltpu.make_async_copy(source, target, load_sem.at[n])
        for n, (source, target) in enumerate(
            (
                (query_hbm, query),
                (key_hbm, key),
                (value_hbm, value),
                (cache_key_hbm, cache_key),
                (cache_value_hbm, cache_value),
            )
        )
    ]
    loads[0].start()

    barrier = pltpu.get_barrier_semaphore()
    pl.semaphore_signal(barrier, inc=1, device_id={"tensor": other}, device_id_type=MESH)

    def greet(d, carry):
        pl.semaphore_signal(barrier, inc=1, device_id={"replica": peer(d)}, device_id_type=MESH)
        return carry

    lax.fori_loop(1, peers, greet, 0)
    tile_lane = lax.broadcasted_iota(jnp.int32, row.shape, 1)
    own_slots = jnp.full(row.shape, -1, jnp.int32)
    for j in range(slots):
        own_slots = jnp.where(tile_lane == j, new_slot_ref[j], own_slots)
    row[...] = own_slots
    tables[0] = own_slots
    pl.semaphore_wait(barrier, peers)

    def table_copy(d):
        return pltpu.make_async_remote_copy(
            src_ref=row,
            dst_ref=tables.at[d],
            send_sem=table_send.at[d],
            recv_sem=table_recv.at[d],
            device_id={"replica": peer(d)},
            device_id_type=MESH,
        )

    lax.fori_loop(1, peers, lambda d, carry: (table_copy(d).start(), carry)[1], 0)

    lane = lax.broadcasted_iota(jnp.int32, (block, LANES), 1)

    def sums_of(ref):
        sums = jnp.zeros((block, LANES), F32)
        for i in range(slots):
            rows = ref[i].astype(F32)
            sums = jnp.where(lane == i, jnp.sum(rows * rows, axis=1, keepdims=True), sums)
        return sums

    def exchange(n):
        return pltpu.make_async_remote_copy(
            src_ref=squares.at[n],
            dst_ref=squares_other.at[n],
            send_sem=square_sem.at[n, 0],
            recv_sem=square_sem.at[n, 1],
            device_id={"tensor": other},
            device_id_type=MESH,
        )

    def normalise(n, ref, gain_ref):
        exchange(n).wait()
        factors = lax.rsqrt((squares[n] + squares_other[n]) / full_width + 1e-06)
        gain = gain_ref[...].astype(F32).reshape(1, width)
        for i in range(slots):
            ref[i] = (ref[i].astype(F32) * factors[:, i : i + 1] * gain).astype(BF16)

    loads[0].wait()
    for load in loads[1:]:
        load.start()
    squares[0] = sums_of(query)
    exchange(0).start()

    lax.fori_loop(1, peers, lambda d, carry: (table_copy(d).wait_recv(), carry)[1], 0)
    board = tables[:, 0, :]
    shape = board.shape
    column = lax.broadcasted_iota(jnp.int32, shape, 1)
    sender = lax.broadcasted_iota(jnp.int32, shape, 0)
    mine = (board >= me * slots) & (board < me * slots + slots)
    chosen = jnp.zeros(shape, jnp.int32)
    places = jnp.zeros(shape, jnp.int32)
    for r in range(capacity):
        first = jnp.min(jnp.where(mine, column, LANES), axis=1, keepdims=True)
        now = mine & (column == first)
        local = jnp.max(jnp.where(now, board - me * slots, 0), axis=1, keepdims=True)
        chosen = jnp.where(column == r, local, chosen)
        places = jnp.where(now, sender * capacity + r, places)
        mine = mine & (column != first)
    sender_vmem[...] = chosen
    sender_scalars = pltpu.make_async_copy(sender_vmem, sender_picks, load_sem.at[5])
    sender_scalars.start()
    normalise(0, query, query_gain_ref)
    sender_scalars.wait()

    def query_copy(d, r):
        return pltpu.make_async_remote_copy(
            src_ref=query_out.at[d, r],
            dst_ref=query_in.at[d, r],
            send_sem=query_send.at[d, r],
            recv_sem=query_recv.at[d, r],
            device_id={"replica": peer(d)},
            device_id_type=MESH,
        )

    def result_copy(d, r):
        return pltpu.make_async_remote_copy(
            src_ref=result_out.at[d, r],
            dst_ref=result_in.at[d, r],
            send_sem=result_send.at[d, r],
            recv_sem=result_recv.at[d, r],
            device_id={"replica": peer(d)},
            device_id_type=MESH,
        )

    def level_copy(d):
        return pltpu.make_async_remote_copy(
            src_ref=level_out.at[d],
            dst_ref=level_in.at[d],
            send_sem=level_send.at[d],
            recv_sem=level_recv.at[d],
            device_id={"replica": peer(d)},
            device_id_type=MESH,
        )

    def send_queries(d, carry):
        for r in range(capacity):
            query_out[d, r] = query[sender_picks[d, r]]
            query_copy(d, r).start()
        return carry

    lax.fori_loop(half, peers, send_queries, 0)
    lax.fori_loop(1, half, send_queries, 0)

    own_row = jnp.broadcast_to(tables[0][0:1], shape)
    back_base = peer(sender) * slots
    theirs = (own_row >= back_base) & (own_row < back_base + slots)
    chosen = jnp.zeros(shape, jnp.int32)
    for r in range(capacity):
        first = jnp.min(jnp.where(theirs, column, LANES), axis=1, keepdims=True)
        chosen = jnp.where(column == r, jnp.where(first == LANES, 0, first), chosen)
        theirs = theirs & (column != first)
    for i in range(slots):
        matching = jnp.where(board == me * slots + i, places, 0)
        place = jnp.max(jnp.max(matching, axis=1, keepdims=True), axis=0, keepdims=True)
        chosen = jnp.where(column == capacity + i, place, chosen)
    picks_vmem[...] = chosen
    scalars = pltpu.make_async_copy(picks_vmem, picks, load_sem.at[6])
    scalars.start()
    loads[1].wait()
    squares[1] = sums_of(key)
    exchange(1).start()
    normalise(1, key, key_gain_ref)
    scalars.wait()
    for load in loads[2:]:
        load.wait()

    cached = cache_key.shape[1]
    position = lax.broadcasted_iota(jnp.int32, (2 * block, cached), 1)
    fold = block // 4

    def visit(d, fetch, target, target_level, before=None, after=None):
        levels = jnp.zeros((block, LANES), F32)
        for r in range(capacity):
            if before is not None:
                before(d, r)
            g = picks[d, r]
            valid = position < lengths_ref[g]
            for c in range(pairs):
                part = slice(c * PAIR, (c + 1) * PAIR)
                result, even, odd = pair_attention(
                    fetch(r, part), cache_key[g, :, part], cache_value[g, :, part], valid
                )
                target[d, r, :, part] = result.astype(BF16)
                levels = jnp.where(lane == 16 * r + 2 * c, even, levels)
                levels = jnp.where(lane == 16 * r + 2 * c + 1, odd, levels)
            if after is not None:
                after(d, r)
        folded = levels[:fold]
        for j in range(1, 4):
            folded = folded + pltpu.roll(levels[j * fold : (j + 1) * fold], 32 * j, 1)
        target_level[d] = folded

    def own_block(i, carry):
        levels = jnp.zeros((block, LANES), F32)
        for c in range(pairs):
            part = slice(c * PAIR, (c + 1) * PAIR)
            result, even, odd = pair_attention(
                query[i, :, part], key[i, :, part], value[i, :, part], None
            )
            own_result[i, :, part] = result
            levels = jnp.where(lane % 16 == 2 * c, even, levels)
            levels = jnp.where(lane % 16 == 2 * c + 1, odd, levels)
        own_level[i] = levels
        return carry

    def combine(d):
        folded = level_in[d]
        levels = jnp.concatenate(
            [folded] + [pltpu.roll(folded, LANES - 32 * j, 1) for j in range(1, 4)], axis=0
        )
        for r in range(capacity):
            i = sender_picks[d, r]
            share = 1.0 / (1.0 + jnp.exp(own_level[i] - levels))
            for h in range(width // HEAD_DIM):
                part = slice(h * HEAD_DIM, (h + 1) * HEAD_DIM)
                own = own_result[i, :, part]
                past = result_in[d, r, :, part].astype(F32)
                at = 16 * r + h
                mixed = own + share[:, at : at + 1] * (past - own)
                result_in[d, r, :, part] = mixed.astype(BF16)

    visit(0, lambda r, part: query[sender_picks[0, r], :, part], result_in, level_in)
    lax.fori_loop(0, slots, own_block, 0)

    def serve(d, carry):
        visit(
            d,
            lambda r, part: query_in[d, r, :, part],
            result_out,
            level_out,
            lambda d, r: query_copy(d, r).wait_recv(),
            lambda d, r: result_copy(d, r).start(),
        )
        level_copy(d).start()
        return carry

    lax.fori_loop(1, peers, serve, 0)
    combine(0)

    def collect(d, carry):
        level_copy(d).wait_recv()
        for r in range(capacity):
            result_copy(d, r).wait_recv()
        combine(d)
        return carry

    lax.fori_loop(1, peers, collect, 0)

    for i in range(slots):
        at = picks[0, capacity + i]
        out_ref[i] = result_in[at // capacity, lax.rem(at, capacity)]

    def finish_sends(d, carry):
        table_copy(d).wait_send()
        level_copy(d).wait_send()
        for r in range(capacity):
            result_copy(d, r).wait_send()
        return carry

    lax.fori_loop(1, peers, finish_sends, 0)

    def finish_queries(d, carry):
        for r in range(capacity):
            query_copy(d, r).wait_send()
        return carry

    lax.fori_loop(1, peers, finish_queries, 0)


def local(
    cache_keys,
    cache_values,
    lengths,
    new_slot,
    query_raw,
    block_keys_raw,
    block_values,
    query_gain,
    key_gain,
):
    slots, block, width = query_raw.shape
    cached = cache_keys.shape[1]
    peers = lax.axis_size("replica")
    capacity = -(-slots // peers)
    full_width = width * lax.axis_size("tensor")
    vmem = pl.BlockSpec(memory_space=pltpu.VMEM)
    smem = pl.BlockSpec(memory_space=pltpu.SMEM)
    hbm = pl.BlockSpec(memory_space=pl.ANY)
    message = (peers, capacity, block, width)
    level = (peers, block // 4, LANES)
    dma = pltpu.SemaphoreType.DMA
    return pl.pallas_call(
        functools.partial(kernel, peers, capacity, full_width),
        out_shape=jax.ShapeDtypeStruct(query_raw.shape, BF16),
        in_specs=[smem, smem, hbm, hbm, hbm, hbm, hbm, vmem, vmem],
        out_specs=vmem,
        scratch_shapes=[
            pltpu.VMEM(query_raw.shape, BF16),
            pltpu.VMEM(query_raw.shape, BF16),
            pltpu.VMEM(query_raw.shape, BF16),
            pltpu.VMEM(cache_keys.shape, BF16),
            pltpu.VMEM(cache_keys.shape, BF16),
            pltpu.VMEM((2, block, LANES), F32),
            pltpu.VMEM((2, block, LANES), F32),
            pltpu.VMEM((8, LANES), jnp.int32),
            pltpu.VMEM((peers, 8, LANES), jnp.int32),
            pltpu.VMEM((peers, LANES), jnp.int32),
            pltpu.SMEM((peers, LANES), jnp.int32),
            pltpu.VMEM((peers, LANES), jnp.int32),
            pltpu.SMEM((peers, LANES), jnp.int32),
            pltpu.VMEM(message, BF16),
            pltpu.VMEM(message, BF16),
            pltpu.VMEM(message, BF16),
            pltpu.VMEM(message, BF16),
            pltpu.VMEM(level, F32),
            pltpu.VMEM(level, F32),
            pltpu.VMEM(query_raw.shape, F32),
            pltpu.VMEM((slots, block, LANES), F32),
            dma((7,)),
            dma((2, 2)),
            dma((peers,)),
            dma((peers,)),
            dma((peers, capacity)),
            dma((peers, capacity)),
            dma((peers, capacity)),
            dma((peers, capacity)),
            dma((peers,)),
            dma((peers,)),
        ],
        compiler_params=pltpu.CompilerParams(
            collective_id=0, has_side_effects=True, vmem_limit_bytes=60 * 1024 * 1024
        ),
        cost_estimate=pl.CostEstimate(
            flops=4 * slots * block * (cached + block) * width,
            bytes_accessed=4 * cache_keys.size + 8 * query_raw.size,
            transcendentals=slots * block * (cached + block) * width // HEAD_DIM,
        ),
    )(
        new_slot,
        lengths,
        query_raw,
        block_keys_raw,
        block_values,
        cache_keys,
        cache_values,
        query_gain,
        key_gain,
    )


def solution(mesh):
    in_specs = (
        P(("groups", "replica"), None, "tensor"),
        P(("groups", "replica"), None, "tensor"),
        P(("groups", "replica")),
        P(("groups", "replica")),
        P(("groups", "replica"), None, "tensor"),
        P(("groups", "replica"), None, "tensor"),
        P(("groups", "replica"), None, "tensor"),
        P("tensor"),
        P("tensor"),
    )
    out_specs = P(("groups", "replica"), None, "tensor")
    return jax.shard_map(local, mesh=mesh, in_specs=in_specs, out_specs=out_specs, check_vma=False)
```

```python
import functools

import jax
import jax.numpy as jnp
from jax import lax
from jax.experimental import pallas as pl
from jax.experimental.pallas import tpu as pltpu
from jax.sharding import PartitionSpec as P

HEAD_DIM = 128
PAIR = 2 * HEAD_DIM
LANES = 128
MESH = pl.DeviceIdType.MESH
F32 = jnp.float32
BF16 = jnp.bfloat16


def pair_attention(queries, keys, values, valid):
    rows = queries.shape[0]
    zeros = jnp.zeros((rows, HEAD_DIM), queries.dtype)
    diagonal = jnp.concatenate(
        [
            jnp.concatenate([queries[:, :HEAD_DIM], zeros], axis=1),
            jnp.concatenate([zeros, queries[:, HEAD_DIM:]], axis=1),
        ],
        axis=0,
    )
    scores = lax.dot_general(
        diagonal, keys, (((1,), (1,)), ((), ())), preferred_element_type=F32
    ) * HEAD_DIM ** (-0.5)
    if valid is not None:
        scores = jnp.where(valid, scores, -1e30)
    top = jnp.max(scores, axis=1, keepdims=True)
    weights = jnp.exp(scores - top)
    total = jnp.sum(weights, axis=1, keepdims=True)
    result = jnp.dot(weights.astype(BF16), values, preferred_element_type=F32)
    inverse = 1.0 / total
    first = result[:rows, :HEAD_DIM] * inverse[:rows]
    second = result[rows:, HEAD_DIM:] * inverse[rows:]
    level = top + jnp.log(total)
    return jnp.concatenate([first, second], axis=1), level[:rows], level[rows:]


def kernel(
    peers,
    capacity,
    full_width,
    new_slot_ref,
    lengths_ref,
    query_hbm,
    key_hbm,
    value_hbm,
    cache_key_hbm,
    cache_value_hbm,
    query_gain_ref,
    key_gain_ref,
    out_ref,
    query,
    key,
    value,
    cache_key,
    cache_value,
    squares,
    squares_other,
    row,
    tables,
    sender_vmem,
    sender_picks,
    picks_vmem,
    picks,
    query_out,
    query_in,
    result_out,
    result_in,
    level_out,
    level_in,
    own_result,
    own_level,
    placed,
    out_sem,
    load_sem,
    square_sem,
    table_send,
    table_recv,
    query_send,
    query_recv,
    result_send,
    result_recv,
    level_send,
    level_recv,
):
    slots, block, width = query.shape
    pairs = width // PAIR
    me = lax.axis_index("replica")
    other = 1 - lax.axis_index("tensor")

    def peer(d):
        partner, bit = 0, 1
        while bit < peers:
            partner = partner + lax.rem(me // bit + d // bit, 2) * bit
            bit *= 2
        return partner

    half, quarter = peers // 2, peers // 4

    loads = [
        pltpu.make_async_copy(source, target, load_sem.at[n])
        for n, (source, target) in enumerate(
            (
                (query_hbm, query),
                (key_hbm, key),
                (value_hbm, value),
                (cache_key_hbm, cache_key),
                (cache_value_hbm, cache_value),
            )
        )
    ]
    loads[0].start()

    barrier = pltpu.get_barrier_semaphore()
    pl.semaphore_signal(barrier, inc=1, device_id={"tensor": other}, device_id_type=MESH)

    def greet(d, carry):
        pl.semaphore_signal(barrier, inc=1, device_id={"replica": peer(d)}, device_id_type=MESH)
        return carry

    lax.fori_loop(1, peers, greet, 0)
    tile_lane = lax.broadcasted_iota(jnp.int32, row.shape, 1)
    own_slots = jnp.full(row.shape, -1, jnp.int32)
    for j in range(slots):
        own_slots = jnp.where(tile_lane == j, new_slot_ref[j], own_slots)
    row[...] = own_slots
    tables[0] = own_slots
    pl.semaphore_wait(barrier, peers)

    def table_copy(d):
        return pltpu.make_async_remote_copy(
            src_ref=row,
            dst_ref=tables.at[d],
            send_sem=table_send.at[d],
            recv_sem=table_recv.at[d],
            device_id={"replica": peer(d)},
            device_id_type=MESH,
        )

    lax.fori_loop(1, peers, lambda d, carry: (table_copy(d).start(), carry)[1], 0)

    lane = lax.broadcasted_iota(jnp.int32, (block, LANES), 1)

    def sums_of(ref):
        sums = jnp.zeros((block, LANES), F32)
        for i in range(slots):
            rows = ref[i].astype(F32)
            sums = jnp.where(lane == i, jnp.sum(rows * rows, axis=1, keepdims=True), sums)
        return sums

    def exchange(n):
        return pltpu.make_async_remote_copy(
            src_ref=squares.at[n],
            dst_ref=squares_other.at[n],
            send_sem=square_sem.at[n, 0],
            recv_sem=square_sem.at[n, 1],
            device_id={"tensor": other},
            device_id_type=MESH,
        )

    def normalise(n, ref, gain_ref):
        exchange(n).wait()
        factors = lax.rsqrt((squares[n] + squares_other[n]) / full_width + 1e-06)
        gain = gain_ref[...].astype(F32).reshape(1, width)
        for i in range(slots):
            ref[i] = (ref[i].astype(F32) * factors[:, i : i + 1] * gain).astype(BF16)

    loads[0].wait()
    for load in loads[1:]:
        load.start()
    squares[0] = sums_of(query)
    exchange(0).start()
    normalise(0, query, query_gain_ref)

    lax.fori_loop(1, peers, lambda d, carry: (table_copy(d).wait_recv(), carry)[1], 0)
    board = tables[:, 0, :]
    shape = board.shape
    column = lax.broadcasted_iota(jnp.int32, shape, 1)
    sender = lax.broadcasted_iota(jnp.int32, shape, 0)
    mine = (board >= me * slots) & (board < me * slots + slots)
    chosen = jnp.zeros(shape, jnp.int32)
    places = jnp.zeros(shape, jnp.int32)
    for r in range(capacity):
        first = jnp.min(jnp.where(mine, column, LANES), axis=1, keepdims=True)
        now = mine & (column == first)
        local = jnp.max(jnp.where(now, board - me * slots, 0), axis=1, keepdims=True)
        chosen = jnp.where(column == r, local, chosen)
        places = jnp.where(now, sender * capacity + r, places)
        mine = mine & (column != first)
    sender_vmem[...] = chosen
    sender_scalars = pltpu.make_async_copy(sender_vmem, sender_picks, load_sem.at[5])
    sender_scalars.start()
    sender_scalars.wait()

    def query_copy(d, r):
        return pltpu.make_async_remote_copy(
            src_ref=query_out.at[d, r],
            dst_ref=query_in.at[d, r],
            send_sem=query_send.at[d, r],
            recv_sem=query_recv.at[d, r],
            device_id={"replica": peer(d)},
            device_id_type=MESH,
        )

    def result_copy(d, r):
        return pltpu.make_async_remote_copy(
            src_ref=result_out.at[d, r],
            dst_ref=result_in.at[d, r],
            send_sem=result_send.at[d, r],
            recv_sem=result_recv.at[d, r],
            device_id={"replica": peer(d)},
            device_id_type=MESH,
        )

    def level_copy(d):
        return pltpu.make_async_remote_copy(
            src_ref=level_out.at[d],
            dst_ref=level_in.at[d],
            send_sem=level_send.at[d],
            recv_sem=level_recv.at[d],
            device_id={"replica": peer(d)},
            device_id_type=MESH,
        )

    def send_queries(d, carry):
        for r in range(capacity):
            query_out[d, r] = query[sender_picks[d, r]]
            query_copy(d, r).start()
        return carry

    lax.fori_loop(half, peers, send_queries, 0)
    lax.fori_loop(1, half, send_queries, 0)

    own_row = jnp.broadcast_to(tables[0][0:1], shape)
    back_base = peer(sender) * slots
    theirs = (own_row >= back_base) & (own_row < back_base + slots)
    chosen = jnp.zeros(shape, jnp.int32)
    for r in range(capacity):
        first = jnp.min(jnp.where(theirs, column, LANES), axis=1, keepdims=True)
        chosen = jnp.where(column == r, jnp.where(first == LANES, 0, first), chosen)
        theirs = theirs & (column != first)
    for i in range(slots):
        matching = jnp.where(board == me * slots + i, places, 0)
        place = jnp.max(jnp.max(matching, axis=1, keepdims=True), axis=0, keepdims=True)
        chosen = jnp.where(column == capacity + i, place, chosen)
    picks_vmem[...] = chosen
    scalars = pltpu.make_async_copy(picks_vmem, picks, load_sem.at[6])
    scalars.start()
    loads[1].wait()
    squares[1] = sums_of(key)
    exchange(1).start()
    normalise(1, key, key_gain_ref)
    scalars.wait()
    for load in loads[2:]:
        load.wait()

    cached = cache_key.shape[1]
    position = lax.broadcasted_iota(jnp.int32, (2 * block, cached), 1)
    fold = block // 4

    def visit(d, fetch, target, target_level, before=None, after=None):
        levels = jnp.zeros((block, LANES), F32)
        for r in range(capacity):
            if before is not None:
                before(d, r)
            g = picks[d, r]
            valid = position < lengths_ref[g]
            for c in range(pairs):
                part = slice(c * PAIR, (c + 1) * PAIR)
                result, even, odd = pair_attention(
                    fetch(r, part), cache_key[g, :, part], cache_value[g, :, part], valid
                )
                target[d, r, :, part] = result.astype(BF16)
                levels = jnp.where(lane == 16 * r + 2 * c, even, levels)
                levels = jnp.where(lane == 16 * r + 2 * c + 1, odd, levels)
            if after is not None:
                after(d, r)
        folded = levels[:fold]
        for j in range(1, 4):
            folded = folded + pltpu.roll(levels[j * fold : (j + 1) * fold], 32 * j, 1)
        target_level[d] = folded

    def own_block(i, carry):
        levels = jnp.zeros((block, LANES), F32)
        for c in range(pairs):
            part = slice(c * PAIR, (c + 1) * PAIR)
            result, even, odd = pair_attention(
                query[i, :, part], key[i, :, part], value[i, :, part], None
            )
            own_result[i, :, part] = result
            levels = jnp.where(lane % 16 == 2 * c, even, levels)
            levels = jnp.where(lane % 16 == 2 * c + 1, odd, levels)
        own_level[i] = levels
        return carry

    def combine(d):
        folded = level_in[d]
        levels = jnp.concatenate(
            [folded] + [pltpu.roll(folded, LANES - 32 * j, 1) for j in range(1, 4)], axis=0
        )
        for r in range(capacity):
            i = sender_picks[d, r]
            share = 1.0 / (1.0 + jnp.exp(own_level[i] - levels))
            for h in range(width // HEAD_DIM):
                part = slice(h * HEAD_DIM, (h + 1) * HEAD_DIM)
                own = own_result[i, :, part]
                past = result_in[d, r, :, part].astype(F32)
                at = 16 * r + h
                mixed = own + share[:, at : at + 1] * (past - own)
                result_in[d, r, :, part] = mixed.astype(BF16)

    visit(0, lambda r, part: query[sender_picks[0, r], :, part], result_in, level_in)
    lax.fori_loop(0, slots, own_block, 0)

    def serve(d, carry):
        visit(
            d,
            lambda r, part: query_in[d, r, :, part],
            result_out,
            level_out,
            lambda d, r: query_copy(d, r).wait_recv(),
            lambda d, r: result_copy(d, r).start(),
        )
        level_copy(d).start()
        return carry

    lax.fori_loop(1, peers, serve, 0)
    combine(0)

    def collect(d, carry):
        level_copy(d).wait_recv()
        for r in range(capacity):
            result_copy(d, r).wait_recv()
        combine(d)
        return carry

    lax.fori_loop(1, peers, collect, 0)

    for i in range(slots):
        at = picks[0, capacity + i]
        placed[i] = result_in[at // capacity, lax.rem(at, capacity)]
        pltpu.make_async_copy(placed.at[i], out_ref.at[i], out_sem.at[i]).start()

    def finish_sends(d, carry):
        table_copy(d).wait_send()
        level_copy(d).wait_send()
        for r in range(capacity):
            result_copy(d, r).wait_send()
        return carry

    lax.fori_loop(1, peers, finish_sends, 0)
    for i in range(slots):
        pltpu.make_async_copy(placed.at[i], out_ref.at[i], out_sem.at[i]).wait()

    def finish_queries(d, carry):
        for r in range(capacity):
            query_copy(d, r).wait_send()
        return carry

    lax.fori_loop(1, peers, finish_queries, 0)


def local(
    cache_keys,
    cache_values,
    lengths,
    new_slot,
    query_raw,
    block_keys_raw,
    block_values,
    query_gain,
    key_gain,
):
    slots, block, width = query_raw.shape
    cached = cache_keys.shape[1]
    peers = lax.axis_size("replica")
    capacity = -(-slots // peers)
    full_width = width * lax.axis_size("tensor")
    vmem = pl.BlockSpec(memory_space=pltpu.VMEM)
    smem = pl.BlockSpec(memory_space=pltpu.SMEM)
    hbm = pl.BlockSpec(memory_space=pl.ANY)
    message = (peers, capacity, block, width)
    level = (peers, block // 4, LANES)
    dma = pltpu.SemaphoreType.DMA
    return pl.pallas_call(
        functools.partial(kernel, peers, capacity, full_width),
        out_shape=jax.ShapeDtypeStruct(query_raw.shape, BF16),
        in_specs=[smem, smem, hbm, hbm, hbm, hbm, hbm, vmem, vmem],
        out_specs=hbm,
        scratch_shapes=[
            pltpu.VMEM(query_raw.shape, BF16),
            pltpu.VMEM(query_raw.shape, BF16),
            pltpu.VMEM(query_raw.shape, BF16),
            pltpu.VMEM(cache_keys.shape, BF16),
            pltpu.VMEM(cache_keys.shape, BF16),
            pltpu.VMEM((2, block, LANES), F32),
            pltpu.VMEM((2, block, LANES), F32),
            pltpu.VMEM((8, LANES), jnp.int32),
            pltpu.VMEM((peers, 8, LANES), jnp.int32),
            pltpu.VMEM((peers, LANES), jnp.int32),
            pltpu.SMEM((peers, LANES), jnp.int32),
            pltpu.VMEM((peers, LANES), jnp.int32),
            pltpu.SMEM((peers, LANES), jnp.int32),
            pltpu.VMEM(message, BF16),
            pltpu.VMEM(message, BF16),
            pltpu.VMEM(message, BF16),
            pltpu.VMEM(message, BF16),
            pltpu.VMEM(level, F32),
            pltpu.VMEM(level, F32),
            pltpu.VMEM(query_raw.shape, F32),
            pltpu.VMEM((slots, block, LANES), F32),
            pltpu.VMEM(query_raw.shape, BF16),
            dma((slots,)),
            dma((7,)),
            dma((2, 2)),
            dma((peers,)),
            dma((peers,)),
            dma((peers, capacity)),
            dma((peers, capacity)),
            dma((peers, capacity)),
            dma((peers, capacity)),
            dma((peers,)),
            dma((peers,)),
        ],
        compiler_params=pltpu.CompilerParams(
            collective_id=0, has_side_effects=True, vmem_limit_bytes=60 * 1024 * 1024
        ),
        cost_estimate=pl.CostEstimate(
            flops=4 * slots * block * (cached + block) * width,
            bytes_accessed=4 * cache_keys.size + 8 * query_raw.size,
            transcendentals=slots * block * (cached + block) * width // HEAD_DIM,
        ),
    )(
        new_slot,
        lengths,
        query_raw,
        block_keys_raw,
        block_values,
        cache_keys,
        cache_values,
        query_gain,
        key_gain,
    )


def solution(mesh):
    in_specs = (
        P(("groups", "replica"), None, "tensor"),
        P(("groups", "replica"), None, "tensor"),
        P(("groups", "replica")),
        P(("groups", "replica")),
        P(("groups", "replica"), None, "tensor"),
        P(("groups", "replica"), None, "tensor"),
        P(("groups", "replica"), None, "tensor"),
        P("tensor"),
        P("tensor"),
    )
    out_specs = P(("groups", "replica"), None, "tensor")
    return jax.shard_map(local, mesh=mesh, in_specs=in_specs, out_specs=out_specs, check_vma=False)
```
